32 devices in a mesh: ctx: 8 (over z, x), head: 2 (over core), exp: 2 (over y).
Axes of the slice: x: 2, y: 2, z: 4, core: 2. Of those that a mesh axis runs over, the one named last changes fastest.
Arguments:
- residual: bfloat16 [1024, 4096], P(('ctx', 'exp')), may hold values from -40 to 40
- queries: bfloat16 [1024, 8192], P('ctx', ('head', 'exp')), may hold values from -5 to 5
- key_head_array: bfloat16 [1024, 512], P('ctx', 'head'), may hold values from -5 to 5
- value_head_array: bfloat16 [1024, 512], P('ctx', 'head'), may hold values from -6 to 6
- doc_ids: int32 [1024], P('ctx'), may hold values from 0 to 7, never falling along the last dimension, each value on 1 to 384 neighbouring positions
- out_weight: bfloat16 [8192, 4096], P(('head', 'exp'), 'ctx'), may hold values from -0.0625 to 0.0625
- norm_gain: float32 [4096], replicated, may hold values from 0.1 to 1.9
- routes: int32 [1024, 8], P(('ctx', 'exp')), may hold values from 0 to 15, all different within a row; in each aligned block of 64 rows (0 to 63, 64 to 127, ...) at most 48 rows name the same one
- gate_probs: float32 [1024, 8], P(('ctx', 'exp')), may hold values from 0.05 to 0.5
- expert_gate: bfloat16 [16, 4096, 768], P(('ctx', 'exp'), None, 'head'), may hold values from -0.09375 to 0.09375
- expert_up: bfloat16 [16, 4096, 768], P(('ctx', 'exp'), None, 'head'), may hold values from -0.09375 to 0.09375
- expert_down: bfloat16 [16, 768, 4096], P(('ctx', 'exp'), 'head'), may hold values from -0.21875 to 0.21875
- grad_out: bfloat16 [1024, 4096], P(('ctx', 'exp')), may hold values from -6 to 6
Outputs:
- layer_out: bfloat16 [1024, 4096], P(('ctx', 'exp'))
- grad_resid: bfloat16 [1024, 4096], P(('ctx', 'exp'))
- grad_queries: bfloat16 [1024, 8192], P('ctx', ('head', 'exp'))
- grad_keys: bfloat16 [1024, 512], P(('ctx', 'exp'), 'head')
- grad_values: bfloat16 [1024, 512], P(('ctx', 'exp'), 'head')
The draws below stay inside these ranges and needn't reach their ends.
Inputs may be any that keep to these rules, and one draw needn't show every extreme that they name: `routes`: each row names 8 different experts; within each aligned block of 64 rows (the rows of one device) no expert is named by more than 48 rows, a bound that some block reaches. `doc_ids`: never falls along the sequence; each document has 1 to 384 tokens and one has exactly 384.
All inputs are finite; a program needn't handle non-finite values.
Results may differ from the reference program's by a relative error of at most 0.024.
Values may be sent and summed in bfloat16 or wider, within the bound.
No kernel may reach another device: no remote copies, remote signals or barrier semaphores. Data moves between devices by JAX's collectives and lax.ppermute only.
A program may use at most 192 MiB of HBM per device.

```python
import math
import jax
import jax.numpy as jnp
import numpy as np
from jax import lax

D = 4096
HEAD_SIZE = 128
QUERY_HEADS = 64
KEY_VALUE_HEADS = 4
TOPK = 8
FF = 768
SPAN = 4
T_CTX = 128
SEQUENCE_TOKENS = 1024
R = 64
EXPERTS = 16
FF_DEV = 384
CAP = 48
DOCMAX = 384
DOCS = 8
N_CTX = 8
N_HEAD = 2
N_EXP = 2


def drawn_parts(key):
    shard_count = jax.random.split(jax.random.fold_in(key, 29), 5)
    return (shard_count[3], shard_count[4])


def draw_residual(key, part):
    shard_count = jax.random.split(jax.random.fold_in(key, 11), 3)
    offset_start = jnp.clip(jax.random.normal(shard_count[0], (SEQUENCE_TOKENS, D), jnp.float32), -4.0, 4.0)
    row_scale = jnp.exp(jax.random.uniform(shard_count[1], (SEQUENCE_TOKENS, 1), jnp.float32, -1.15, 1.15))
    col_scale = jnp.exp(jax.random.uniform(shard_count[2], (1, D), jnp.float32, -1.15, 1.15))
    return jnp.clip(offset_start * row_scale * col_scale, -40.0, 40.0).astype(jnp.bfloat16)


def draw_key_head_array(key, part):
    query_key, random_key_seed = drawn_parts(key)
    offset_start = jnp.clip(jax.random.normal(random_key_seed, (SEQUENCE_TOKENS, KEY_VALUE_HEADS * HEAD_SIZE), jnp.float32), -4.0, 4.0)
    return offset_start.astype(jnp.bfloat16)


def draw_queries(key, part):
    query_key, random_key_seed = drawn_parts(key)
    offset_start = jnp.clip(jax.random.normal(query_key, (SEQUENCE_TOKENS, QUERY_HEADS * HEAD_SIZE), jnp.float32), -4.0, 4.0)
    return offset_start.astype(jnp.bfloat16)


def level_of(stream_key, shape, cuts, least, top_value):
    level = 1.0
    for position, shards_of in cuts:
        heights = jax.random.uniform(jax.random.fold_in(jax.random.fold_in(stream_key, 6), position), (shards_of,), jnp.float32, least / len(cuts), top_value / len(cuts))
        level = level * jnp.repeat(jnp.exp(heights), shape[position] // shards_of).reshape((-1,) + (1,) * (len(shape) - 1 - position))
    return level


def split_up(amount, total, bound, skew):
    portions = [(1 << 20) // math.isqrt(grade ** skew) + 1 for grade in range(2, amount + 1)]
    surplus, counts = total - bound - (amount - 1), [1] * (amount - 1)
    while surplus > 0:
        free = [i for i in range(amount - 1) if counts[i] < bound]
        mass, left = sum([portions[i] for i in free]), surplus
        for i in free:
            addition = min(bound - counts[i], max(1, left * portions[i] // mass), surplus)
            counts[i] = counts[i] + addition
            surplus = surplus - addition
    return np.array([bound] + counts)


def ragged(key, amount, total, bound, lean):
    if amount == 2:
        one = jax.random.randint(key, (), max(1, total - bound), min(bound, total - 1) + 1)
        return jnp.stack([one, total - one])
    sizes = jnp.asarray(split_up(amount, total, bound, lean), jnp.int32)
    pairs = (amount - 1) // 2
    donor, sink = sizes[1:1 + 2 * pairs:2], sizes[2:2 + 2 * pairs:2]
    room = jnp.minimum(donor - 1, bound - sink)
    passed = jax.random.randint(jax.random.fold_in(key, 1), (pairs,), 0, 1 << 20) % (room + 1)
    sizes = sizes.at[1:1 + 2 * pairs:2].set(donor - passed).at[2:2 + 2 * pairs:2].set(sink + passed)
    return sizes[jax.random.permutation(jax.random.fold_in(key, 2), amount)]


def deal_out(rng, own, number, rows, number_of, top, most, lean):
    ranking = jax.random.permutation(rng, number_of)
    packed, usual = portions_of(number_of, rows * top, most, lean, True), portions_of(number_of, rows * top, most, lean, False)
    places = jnp.arange(number_of)

    def named(tallies, offset_by):
        used = int((tallies > 0).sum())
        fixed = max(1, used // 4)
        moved = fixed + (places - fixed + offset_by * (used - fixed)) % max(1, number_of - fixed)
        return jnp.zeros((number_of,), jnp.int32).at[ranking[jnp.where(places < fixed, places, moved)]].set(jnp.asarray(tallies, jnp.int32))

    tallies = jnp.where(number % 4 == 0, named(packed, number // 4), named(usual, number - number // 4 - 1))
    mixed = jax.random.permutation(jax.random.fold_in(own, 3), number_of)
    source_of, taker = mixed[0:number_of // 2 * 2:2], mixed[1:number_of // 2 * 2:2]
    margin = jnp.minimum(tallies[source_of] - 1, most - tallies[taker]) // 2
    margin = jnp.where((source_of == ranking[0]) | (taker == ranking[0]) | (tallies[taker] == 0), 0, jnp.maximum(margin, 0))
    moved = jax.random.randint(jax.random.fold_in(own, 4), (number_of // 2,), 0, 1 << 20) % (margin + 1)
    tallies = tallies.at[source_of].add(-moved).at[taker].add(moved)
    labels = jnp.searchsorted(jnp.cumsum(tallies), jnp.arange(rows * top), side="right").astype(jnp.int32)
    table = labels.reshape(top, rows).T
    table = table[jax.random.permutation(jax.random.fold_in(own, 1), rows)]
    offset_by = jax.random.randint(jax.random.fold_in(own, 2), (rows, 1), 0, top)
    return jnp.take_along_axis(table, (jnp.arange(top)[None, :] + offset_by) % top, axis=1)


def portions_of(amount, total, most, skew, full):
    portions = [(1 << 20) // math.isqrt(standing ** skew) + 1 for standing in range(1, amount + 1)]
    largest = most if full else min(most, max(-(-total // amount), total * portions[0] // sum(portions)))
    least = 1 if total - largest >= amount - 1 else 0
    counts, rest = [largest] + [least] * (amount - 1), total - largest - least * (amount - 1)
    while rest > 0:
        candidates = [i for i in range(1, amount) if counts[i] < largest] or [i for i in range(1, amount) if counts[i] < most]
        pool, left = sum([portions[i] for i in candidates]), rest
        for i in candidates:
            more = min(most - counts[i], max(1, left * portions[i] // pool), rest)
            counts[i] = counts[i] + more
            rest = rest - more
    return np.array(counts)


def scatter_about(rng, dims, scale, most, cuts=(), kind=jnp.bfloat16):
    loudness = level_of(rng, dims, cuts, -0.22, 0.18) if cuts else 1.0
    values = jax.random.normal(rng, dims, jnp.float32) * scale * loudness
    return jnp.minimum(jnp.maximum(values, -most), most).astype(kind)


def setup_inputs(seed: int = 0) -> dict:
    arg_keys = jax.random.split(jax.random.key(seed), 14)
    residual = draw_residual(jax.random.fold_in(arg_keys[13], 71), 0)
    queries = draw_queries(jax.random.fold_in(arg_keys[13], 71), 0)
    key_head_array = draw_key_head_array(jax.random.fold_in(arg_keys[13], 71), 0)
    value_head_array = scatter_about(arg_keys[3], (SEQUENCE_TOKENS, KEY_VALUE_HEADS * HEAD_SIZE), 1.0, 6.0, ((0, 8), (1, 2)))
    doc_ids = jnp.searchsorted(jnp.cumsum(ragged(arg_keys[4], DOCS, SEQUENCE_TOKENS, DOCMAX, 2)), jnp.arange(SEQUENCE_TOKENS), side="right").astype(jnp.int32)
    out_weight = scatter_about(arg_keys[5], (QUERY_HEADS * HEAD_SIZE, D), (QUERY_HEADS * HEAD_SIZE) ** -0.5, 0.0625, ((0, 4), (1, 8)))
    norm_gain = jnp.clip(1.0 + 0.18 * jax.random.normal(arg_keys[6], (D,), jnp.float32), 0.1, 1.9)
    routes_keys = jax.random.split(jax.random.fold_in(arg_keys[7], 1), SEQUENCE_TOKENS // R)
    routes_turns = jax.random.permutation(jax.random.fold_in(arg_keys[7], 3), SEQUENCE_TOKENS // R)
    routes = jax.vmap(lambda own, number: deal_out(jax.random.fold_in(arg_keys[7], 2), own, number, R, EXPERTS, TOPK, CAP, 2))(routes_keys, routes_turns).reshape((SEQUENCE_TOKENS, TOPK))
    gate_probs = jnp.clip(jnp.exp(math.log(0.5) - 2.3025851 * jax.random.uniform(arg_keys[8], (SEQUENCE_TOKENS, TOPK), jnp.float32) ** level_of(arg_keys[8], (SEQUENCE_TOKENS, TOPK), ((0, 16),), -0.2, 0.2)), 0.05, 0.5)
    expert_gate = scatter_about(arg_keys[9], (EXPERTS, D, FF), D ** -0.5, 0.09375, ((0, 16), (2, 2)))
    expert_up = scatter_about(arg_keys[10], (EXPERTS, D, FF), D ** -0.5, 0.09375, ((0, 16), (2, 2)))
    expert_down = scatter_about(arg_keys[11], (EXPERTS, FF, D), FF ** -0.5, 0.21875, ((0, 16), (1, 2)))
    grad_out = scatter_about(arg_keys[12], (SEQUENCE_TOKENS, D), 1.0, 6.0, ((0, 16),))
    return dict(residual=residual, queries=queries, key_head_array=key_head_array, value_head_array=value_head_array, doc_ids=doc_ids, out_weight=out_weight, norm_gain=norm_gain, routes=routes, gate_probs=gate_probs, expert_gate=expert_gate, expert_up=expert_up, expert_down=expert_down, grad_out=grad_out)


neg_large = -1e+30
eps_norm = 1e-06

def rms_normed(hidden, norm_gain):
    factor = lax.rsqrt(lax.optimization_barrier(jnp.mean(hidden * hidden, axis=-1, keepdims=True)) + eps_norm)
    return hidden * factor * norm_gain

def rounded(values):
    return lax.optimization_barrier(values.astype(jnp.bfloat16)).astype(jnp.float32)

def reference(residual, queries, key_head_array, value_head_array, doc_ids, out_weight, norm_gain, routes, gate_probs, expert_gate, expert_up, expert_down, grad_out):
    group_width = QUERY_HEADS // KEY_VALUE_HEADS
    score_scale = 1.0 / math.sqrt(HEAD_SIZE)
    window_extent = (SPAN - 1) * T_CTX
    layer_window = SPAN * T_CTX
    padded_keys = jnp.concatenate([jnp.zeros((window_extent, KEY_VALUE_HEADS * HEAD_SIZE), jnp.bfloat16), key_head_array], axis=0)
    padded_values = jnp.concatenate([jnp.zeros((window_extent, KEY_VALUE_HEADS * HEAD_SIZE), jnp.bfloat16), value_head_array], axis=0)
    doc_pad = jnp.concatenate([jnp.full((window_extent,), -1, jnp.int32), doc_ids.astype(jnp.int32)], axis=0)

    def block_inputs(block):
        begin_offset = (block * T_CTX).astype(jnp.int32)
        query_block = lax.dynamic_slice_in_dim(queries, begin_offset, T_CTX, 0).astype(jnp.float32).reshape(T_CTX, QUERY_HEADS, HEAD_SIZE)
        windowed_keys = lax.dynamic_slice_in_dim(padded_keys, begin_offset, layer_window, 0).astype(jnp.float32).reshape(layer_window, KEY_VALUE_HEADS, 1, HEAD_SIZE)
        repeated_keys = jnp.broadcast_to(windowed_keys, (layer_window, KEY_VALUE_HEADS, group_width, HEAD_SIZE)).reshape(layer_window, QUERY_HEADS, HEAD_SIZE)
        windowed_values = lax.dynamic_slice_in_dim(padded_values, begin_offset, layer_window, 0).astype(jnp.float32).reshape(layer_window, KEY_VALUE_HEADS, 1, HEAD_SIZE)
        repeated_values = jnp.broadcast_to(windowed_values, (layer_window, KEY_VALUE_HEADS, group_width, HEAD_SIZE)).reshape(layer_window, QUERY_HEADS, HEAD_SIZE)
        query_docs = lax.dynamic_slice_in_dim(doc_ids.astype(jnp.int32), begin_offset, T_CTX, 0)
        key_docs = lax.dynamic_slice_in_dim(doc_pad, begin_offset, layer_window, 0)
        query_pos = begin_offset + jnp.arange(T_CTX, dtype=jnp.int32)
        key_pos = begin_offset - window_extent + jnp.arange(layer_window, dtype=jnp.int32)
        visible = (query_docs[:, None] == key_docs[None, :]) & (key_pos[None, :] <= query_pos[:, None]) & (key_pos[None, :] >= 0)
        scores = jnp.einsum('qhd,khd->qhk', query_block, repeated_keys) * score_scale
        scores = jnp.where(visible[:, None, :], scores, neg_large)
        return (query_block, repeated_keys, repeated_values, scores)

    def forward_block(block):
        query_block, repeated_keys, repeated_values, scores = block_inputs(block)
        row_max = lax.optimization_barrier(jnp.max(scores, axis=-1))
        weights = jnp.exp(scores - row_max[..., None])
        row_total = lax.optimization_barrier(jnp.sum(weights, axis=-1))
        mixed = jnp.einsum('qhk,khd->qhd', rounded(weights), repeated_values) / row_total[..., None]
        return (mixed.astype(jnp.bfloat16).reshape(T_CTX, QUERY_HEADS * HEAD_SIZE), row_max + jnp.log(row_total))
    attn_blocks, lse = lax.map(forward_block, jnp.arange(N_CTX, dtype=jnp.int32))
    attn = attn_blocks.reshape(SEQUENCE_TOKENS, QUERY_HEADS * HEAD_SIZE)
    attn_proj = jnp.dot(attn, out_weight, preferred_element_type=jnp.float32)
    hidden = residual.astype(jnp.float32) + attn_proj
    normed_full, pullback = jax.vjp(lambda values: rms_normed(values, norm_gain), hidden)
    normed = normed_full.astype(jnp.bfloat16)
    limit = N_CTX * N_EXP * CAP
    flat_routes = routes.reshape(-1).astype(jnp.int32)
    flat_gates = gate_probs.reshape(-1)

    def expert_step(carry, inputs):
        moe_sum, norm_grad = carry
        gate_mat, up_mat, down_mat, expert_index = inputs
        chosen = flat_routes == expert_index
        picks = jnp.nonzero(chosen, size=limit, fill_value=0)[0].astype(jnp.int32)
        live_rows = jnp.arange(limit, dtype=jnp.int32) < jnp.sum(chosen.astype(jnp.int32))
        token_ids = picks // TOPK
        route_weight = jnp.where(live_rows, flat_gates[picks], 0.0)
        rows_in = normed[token_ids]
        rows_grad = grad_out[token_ids]
        gate_pre = jnp.dot(rows_in, gate_mat, preferred_element_type=jnp.float32)
        up_pre = jnp.dot(rows_in, up_mat, preferred_element_type=jnp.float32)
        sigma = jax.nn.sigmoid(gate_pre)
        silu_val = gate_pre * sigma
        act = rounded(silu_val * up_pre).reshape(limit, N_HEAD, FF_DEV)
        parts_out = jnp.einsum('rpf,pfd->rpd', act, down_mat.astype(jnp.float32).reshape(N_HEAD, FF_DEV, D))
        expert_out = lax.optimization_barrier(jnp.sum(rounded(parts_out), axis=1))
        back_act = jnp.dot(rows_grad, down_mat.T, preferred_element_type=jnp.float32)
        slope = sigma * (1.0 + gate_pre * (1.0 - sigma))
        grad_gate = rounded(back_act * up_pre * slope).reshape(limit, N_HEAD, FF_DEV)
        grad_up = rounded(back_act * silu_val).reshape(limit, N_HEAD, FF_DEV)
        parts_back = jnp.einsum('rpf,dpf->rpd', grad_gate, gate_mat.astype(jnp.float32).reshape(D, N_HEAD, FF_DEV))
        parts_back = parts_back + jnp.einsum('rpf,dpf->rpd', grad_up, up_mat.astype(jnp.float32).reshape(D, N_HEAD, FF_DEV))
        expert_back = lax.optimization_barrier(jnp.sum(rounded(parts_back), axis=1))
        moe_sum = moe_sum.at[token_ids].add(route_weight[:, None] * expert_out)
        norm_grad = norm_grad.at[token_ids].add(route_weight[:, None] * expert_back)
        return ((moe_sum, norm_grad), None)
    start_carry = (jnp.zeros((SEQUENCE_TOKENS, D), jnp.float32), jnp.zeros((SEQUENCE_TOKENS, D), jnp.float32))
    expert_ids = jnp.arange(EXPERTS, dtype=jnp.int32)
    (moe_sum, norm_grad), unused = lax.scan(expert_step, start_carry, (expert_gate, expert_up, expert_down, expert_ids))
    layer_out = (hidden + moe_sum).astype(jnp.bfloat16)
    grad_hidden = grad_out.astype(jnp.float32) + pullback(norm_grad)[0]
    grad_resid = grad_hidden.astype(jnp.bfloat16)
    grad_attn = jnp.dot(grad_resid, out_weight.T, preferred_element_type=jnp.float32).astype(jnp.bfloat16)

    def backward_block(carry, block):
        key_acc, value_acc = carry
        query_block, repeated_keys, repeated_values, scores = block_inputs(block)
        begin_offset = (block * T_CTX).astype(jnp.int32)
        attn_block = lax.dynamic_slice_in_dim(attn, begin_offset, T_CTX, 0).astype(jnp.float32).reshape(T_CTX, QUERY_HEADS, HEAD_SIZE)
        grad_block = lax.dynamic_slice_in_dim(grad_attn, begin_offset, T_CTX, 0).astype(jnp.float32).reshape(T_CTX, QUERY_HEADS, HEAD_SIZE)
        delta = lax.optimization_barrier(jnp.sum(grad_block * attn_block, axis=-1))
        probs = jnp.exp(scores - lse[block][..., None])
        grad_weights = jnp.einsum('qhd,khd->qhk', grad_block, repeated_values)
        dscore = rounded(probs * (grad_weights - delta[..., None]))
        grad_query = jnp.einsum('qhk,khd->qhd', dscore, repeated_keys) * score_scale
        key_gradient = jnp.einsum('qhk,qhd->khd', dscore, query_block) * score_scale
        key_gradient = lax.optimization_barrier(jnp.sum(key_gradient.reshape(layer_window, KEY_VALUE_HEADS, group_width, HEAD_SIZE), axis=2)).reshape(layer_window, KEY_VALUE_HEADS * HEAD_SIZE)
        value_gradient = jnp.einsum('qhk,qhd->khd', rounded(probs), grad_block)
        value_gradient = lax.optimization_barrier(jnp.sum(value_gradient.reshape(layer_window, KEY_VALUE_HEADS, group_width, HEAD_SIZE), axis=2)).reshape(layer_window, KEY_VALUE_HEADS * HEAD_SIZE)
        key_acc = lax.dynamic_update_slice_in_dim(key_acc, lax.dynamic_slice_in_dim(key_acc, begin_offset, layer_window, 0) + key_gradient, begin_offset, 0)
        value_acc = lax.dynamic_update_slice_in_dim(value_acc, lax.dynamic_slice_in_dim(value_acc, begin_offset, layer_window, 0) + value_gradient, begin_offset, 0)
        return ((key_acc, value_acc), grad_query.astype(jnp.bfloat16).reshape(T_CTX, QUERY_HEADS * HEAD_SIZE))
    gradient_begin = (jnp.zeros((window_extent + SEQUENCE_TOKENS, KEY_VALUE_HEADS * HEAD_SIZE), jnp.float32), jnp.zeros((window_extent + SEQUENCE_TOKENS, KEY_VALUE_HEADS * HEAD_SIZE), jnp.float32))
    (key_acc, value_acc), query_blocks = lax.scan(backward_block, gradient_begin, jnp.arange(N_CTX, dtype=jnp.int32))
    grad_queries = query_blocks.reshape(SEQUENCE_TOKENS, QUERY_HEADS * HEAD_SIZE)
    grad_keys = key_acc[window_extent:].astype(jnp.bfloat16)
    grad_values = value_acc[window_extent:].astype(jnp.bfloat16)
    return (layer_out, grad_resid, grad_queries, grad_keys, grad_values)
```

```python
import math

import jax
import jax.numpy as jnp
from jax import lax
from jax.experimental import pallas as pl
from jax.experimental.pallas import tpu as pltpu
from jax.sharding import PartitionSpec as P

HEAD_SIZE = 128
QUERY_HEADS = 64
KEY_VALUE_HEADS = 4
SPAN = 4


neg_large = -1e30
eps_norm = 1e-06
bf16 = jnp.bfloat16
f32 = jnp.float32
SCALE = 1.0 / math.sqrt(HEAD_SIZE)
LAST = (((1,), (1,)), ((), ()))
FIRST = (((0,), (0,)), ((), ()))


def dot(a, b, dims=None):
    if dims is None:
        return jnp.dot(a, b, preferred_element_type=f32)
    return lax.dot_general(a, b, dims, preferred_element_type=f32)


def attend_forward(q_ref, k_ref, v_ref, bias_ref, attn_ref, lse_ref):
    keys, values, bias = k_ref[...], v_ref[...], bias_ref[...]
    totals = []
    for head in range(q_ref.shape[1] // HEAD_SIZE):
        part = slice(head * HEAD_SIZE, (head + 1) * HEAD_SIZE)
        scores = dot(q_ref[:, part], keys, LAST) * SCALE + bias
        top = jnp.max(scores, axis=-1, keepdims=True)
        weights = jnp.exp(scores - top)
        total = jnp.sum(weights, axis=-1, keepdims=True)
        attn_ref[:, part] = (dot(weights.astype(bf16), values) / total).astype(bf16)
        totals.append(top + jnp.log(total))
    lse_ref[...] = jnp.concatenate(totals, axis=1)


def attend_backward(
    q_ref, k_ref, v_ref, bias_ref, attn_ref, lse_ref, grad_ref, dq_ref, dk_ref, dv_ref
):
    keys, values, bias = k_ref[...], v_ref[...], bias_ref[...]
    dk_ref[...] = jnp.zeros_like(dk_ref)
    dv_ref[...] = jnp.zeros_like(dv_ref)
    for head in range(q_ref.shape[1] // HEAD_SIZE):
        part = slice(head * HEAD_SIZE, (head + 1) * HEAD_SIZE)
        query, grad = q_ref[:, part], grad_ref[:, part]
        delta = jnp.sum(
            grad.astype(f32) * attn_ref[:, part].astype(f32), axis=-1, keepdims=True
        )
        scores = dot(query, keys, LAST) * SCALE + bias
        probs = jnp.exp(scores - lse_ref[:, head : head + 1])
        dscore = (probs * (dot(grad, values, LAST) - delta)).astype(bf16)
        dq_ref[:, part] = (dot(dscore, keys) * SCALE).astype(bf16)
        dk_ref[...] += dot(dscore, query, FIRST)
        dv_ref[...] += dot(probs.astype(bf16), grad, FIRST)
    dk_ref[...] = dk_ref[...] * SCALE


def run_kernel(body, outs, args, flops):
    moved = sum(a.size * a.dtype.itemsize for a in (*args, *outs))
    return pl.pallas_call(
        body,
        out_shape=outs,
        compiler_params=pltpu.CompilerParams(vmem_limit_bytes=40 * 2**20),
        cost_estimate=pl.CostEstimate(flops=flops, bytes_accessed=moved, transcendentals=0),
    )(*args)


def local(
    residual,
    queries,
    key_head_array,
    value_head_array,
    doc_ids,
    out_weight,
    norm_gain,
    routes,
    gate_probs,
    expert_gate,
    expert_up,
    expert_down,
    grad_out,
):
    C, H, E = lax.axis_size("ctx"), lax.axis_size("head"), lax.axis_size("exp")
    c, h, e = lax.axis_index("ctx"), lax.axis_index("head"), lax.axis_index("exp")
    tokens, features = queries.shape
    head_count = features // HEAD_SIZE
    group_width = QUERY_HEADS // KEY_VALUE_HEADS
    rows, width = residual.shape
    r = rows // H
    cols = width // C
    half = C // 2

    cycle = list(range(0, C, 2)) + list(range(C - 1, 0, -2))
    places = [cycle.index(i) for i in range(C)]
    ahead = [(cycle[i], cycle[(i + 1) % C]) for i in range(C)]
    back = [(d, s) for s, d in ahead]
    place = jnp.asarray(places, jnp.int32)[c]
    cycle_array = jnp.asarray(cycle, jnp.int32)

    def owner(k):
        return cycle_array[lax.rem(place + k + C, C)]

    def to_ahead(x):
        return lax.ppermute(x, "ctx", ahead)

    def to_back(x):
        return lax.ppermute(x, "ctx", back)

    def to_core(x):
        return lax.ppermute(x, "head", [(i, (i + 1) % H) for i in range(H)])

    def exp_from(x, j):
        return lax.ppermute(x, "exp", [((i + j) % E, i) for i in range(E)])

    def exp_to(x, j):
        return lax.ppermute(x, "exp", [(i, (i + j) % E) for i in range(E)])

    def take(x, i, axis=0):
        return lax.dynamic_index_in_dim(x, i, axis, keepdims=False)

    def ring_gather(x):
        found = {0: x}
        f = b = x
        for k in range(1, half):
            f, b = to_ahead(f), to_back(b)
            found[-k], found[k] = f, b
        n = x.shape[0] // 2
        found[half] = jnp.concatenate([to_ahead(f[:n]), to_back(b[n:])], axis=0)
        return found

    def ring_reduce(part):
        far = part(half).astype(bf16)
        n = far.shape[0] // 2
        f, b = to_ahead(far[:n]), to_back(far[n:])
        for k in range(half - 1, 0, -1):
            own_f, own_b = part(k), part(-k)
            if k == half - 1:
                own_f = jnp.concatenate([own_f[:n] + f, own_f[n:]], axis=0)
                own_b = jnp.concatenate([own_b[:n], own_b[n:] + b], axis=0)
            else:
                own_f, own_b = own_f + f, own_b + b
            f, b = to_ahead(own_f.astype(bf16)), to_back(own_b.astype(bf16))
        return part(0) + f + b

    def placed(found, axis=0):
        out = None
        for k, x in found.items():
            x = jnp.expand_dims(x, axis)
            if out is None:
                shape = list(x.shape)
                shape[axis] = C
                out = jnp.zeros(shape, x.dtype)
            out = lax.dynamic_update_slice_in_dim(out, x, owner(k), axis)
        return out

    pair_index = e * head_count // group_width
    own_keys = lax.dynamic_slice_in_dim(key_head_array, pair_index * HEAD_SIZE, HEAD_SIZE, 1)
    own_values = lax.dynamic_slice_in_dim(value_head_array, pair_index * HEAD_SIZE, HEAD_SIZE, 1)
    docs_rows = jnp.broadcast_to(doc_ids.astype(bf16)[None, :], (16, tokens))
    payload = jnp.concatenate([own_keys, own_values, docs_rows], axis=0)
    blocks = [payload] + [
        lax.ppermute(payload, "ctx", [(i, (i + d) % C) for i in range(C)]) for d in range(1, SPAN)
    ]
    keys = jnp.concatenate([b[:tokens] for b in blocks], axis=0)
    values = jnp.concatenate([b[tokens : 2 * tokens] for b in blocks], axis=0)
    key_docs = jnp.concatenate([b[2 * tokens] for b in blocks], axis=0)
    key_pos = jnp.concatenate(
        [(c - d) * tokens + jnp.arange(tokens, dtype=jnp.int32) for d in range(SPAN)]
    )
    query_pos = c * tokens + jnp.arange(tokens, dtype=jnp.int32)
    visible = (
        (doc_ids.astype(bf16)[:, None] == key_docs[None, :])
        & (key_pos[None, :] <= query_pos[:, None])
        & (key_pos[None, :] >= 0)
    )
    bias = jnp.where(visible, 0.0, neg_large).astype(f32)

    gate_mat, up_mat, down_mat = expert_gate[0], expert_up[0], expert_down[0]
    into = jnp.concatenate([gate_mat, to_core(gate_mat), up_mat, to_core(up_mat)], axis=1)
    down = jnp.concatenate([down_mat, to_core(down_mat)], axis=0)
    ff = down.shape[0]

    own_grad_out = take(grad_out.reshape(H, r, width), h)
    grads_own = placed(ring_gather(own_grad_out)).reshape(C * r, width)
    grads = [grads_own] + [exp_from(grads_own, j) for j in range(1, E)]

    expert_count = C * E
    own_routes = take(routes.reshape(H, r, -1), h)
    own_gates = take(gate_probs.reshape(H, r, -1), h)
    chosen = own_routes[:, :, None] == jnp.arange(expert_count, dtype=jnp.int32)
    table = jnp.sum(jnp.where(chosen, own_gates[:, :, None], 0.0), axis=1)
    table = lax.all_gather(table, ("ctx", "exp"), axis=0, tiled=False).reshape(C, E, r, expert_count)
    gates = take(table, c * E + e, 3)
    gates = jnp.roll(jnp.swapaxes(gates, 0, 1), -e, axis=0).reshape(E * C * r, 1)

    own_residual = take(residual.reshape(H, r, C, cols), h)
    residual_cols = lax.all_to_all(jnp.swapaxes(own_residual, 0, 1), "ctx", 0, 0, tiled=True)

    attn, lse = run_kernel(
        attend_forward,
        (
            jax.ShapeDtypeStruct((tokens, features), bf16),
            jax.ShapeDtypeStruct((tokens, head_count), f32),
        ),
        (queries, keys, values, bias),
        4 * tokens * keys.shape[0] * features,
    )

    projected = placed({k: dot(x, out_weight) for k, x in ring_gather(attn).items()})
    projected = projected.reshape(C, E, H, r, cols)
    share = take(projected, h, 2) + to_core(take(projected, 1 - h, 2).astype(bf16))
    attn_proj = take(share, e, 1)
    for j in range(1, E):
        attn_proj = attn_proj + exp_to(take(share, lax.rem(e + j, E), 1).astype(bf16), j)
    hidden = residual_cols.astype(f32) + attn_proj
    gain = lax.dynamic_slice_in_dim(norm_gain, c * cols, cols, 0)
    scaled = (hidden * gain).astype(bf16).reshape(C * r, cols)

    def summed(x):
        return jnp.roll(lax.psum(jnp.roll(x, e, axis=0), ("ctx", "exp")), -e, axis=0)

    squares = jnp.sum(hidden * hidden, axis=-1).reshape(1, C * r)
    squares = summed(jnp.concatenate([squares, jnp.zeros((E - 1, C * r), f32)], axis=0))
    factor = lax.rsqrt(squares / width + eps_norm).reshape(E * C * r, 1)

    found = ring_gather(scaled)
    gathered = [placed(found, 1)]
    near = 1 if half > 2 else 0
    for j in range(1, E):
        if E > 2:
            gathered.append(exp_from(gathered[0], j))
            continue
        first = exp_from(scaled, j)
        others = {k: exp_from(x, j) for k, x in found.items() if abs(k) > near}
        others[0] = first
        if near:
            others[-1], others[1] = to_ahead(first), to_back(first)
        gathered.append(placed(others, 1))
    rows_in = jnp.concatenate(gathered, axis=0).reshape(E * C * r, width)
    rows_grad = jnp.concatenate(grads, axis=0)

    pre = dot(rows_in, into)
    gate_raw, up_raw = pre[:, :ff], pre[:, ff:]
    gate_pre, up_pre = gate_raw * factor, up_raw * factor
    sigma = jax.nn.sigmoid(gate_pre)
    silu_val = gate_pre * sigma
    act = (gates * silu_val * up_pre).astype(bf16)
    back_act = gates * dot(rows_grad, down, LAST)
    slope = sigma * (1.0 + gate_pre * (1.0 - sigma))
    grad_gate = (back_act * up_pre * slope).astype(bf16)
    grad_up = (back_act * silu_val).astype(bf16)
    inner = jnp.sum(grad_gate.astype(f32) * gate_raw + grad_up.astype(f32) * up_raw, axis=-1)
    inner = summed(inner.reshape(E, C * r))[0].reshape(C, r, 1)
    grad_both = jnp.concatenate([grad_gate, grad_up], axis=1)

    def back_part(k):
        weight = lax.dynamic_slice_in_dim(into, owner(k) * cols, cols, 0)
        return dot(grad_both, weight, LAST).reshape(E, C * r, cols)

    back_parts = {k: back_part(k) for k in range(1 - half, half + 1)}
    sums = {k: x[0] for k, x in back_parts.items()}
    for j in range(1, E):
        others = {k: x[j].astype(bf16) for k, x in back_parts.items()}
        if E > 2:
            moved = exp_to(jnp.stack(list(others.values())), j)
            sums = {k: sums[k] + moved[i] for i, k in enumerate(others)}
            continue
        for k in others:
            if abs(k) > near:
                sums[k] = sums[k] + exp_to(others[k], j)
        last = back_parts[0][j]
        if near:
            last = last + to_ahead(others[1]) + to_back(others[-1])
        sums[0] = sums[0] + exp_to(last.astype(bf16), j)
    norm_grad = ring_reduce(lambda k: sums[k]).reshape(C, r, cols)

    own_factor = factor[: C * r].reshape(C, r, 1)
    grad_hidden = (
        take(grads_own.reshape(C, r, C, cols), c, 2).astype(f32)
        + own_factor * gain * norm_grad
        - hidden * (own_factor * own_factor * own_factor * inner / width)
    )
    grad_cols = grad_hidden.astype(bf16)

    outs = dot(act, down).reshape(E, C * r, width)
    out_sum = outs[0]
    for j in range(1, E):
        out_sum = out_sum + exp_to(outs[j].astype(bf16), j)
    out_sum = out_sum.reshape(C, r, width)
    moe_rows = ring_reduce(lambda k: take(out_sum, owner(k)))

    grad_exp = jnp.stack([grad_cols] + [exp_from(grad_cols, j) for j in range(1, E)], axis=1)
    grad_exp = jnp.roll(grad_exp, e, axis=1)
    grad_other = to_core(grad_exp)
    grad_rows = jnp.roll(jnp.stack([grad_exp, grad_other], axis=2), h, axis=2)
    grad_rows = grad_rows.reshape(C, tokens, cols)
    grad_attn = ring_reduce(lambda k: dot(take(grad_rows, owner(k)), out_weight, LAST)).astype(bf16)

    pair = jnp.stack([attn_proj.astype(bf16), grad_cols], axis=1)
    pair = jnp.moveaxis(lax.all_to_all(pair, "ctx", 0, 0, tiled=True), 0, 2).reshape(2, r, width)
    hidden_rows = take(residual.reshape(H, r, width), h).astype(f32) + pair[0].astype(f32)
    layer_rows = (hidden_rows + moe_rows).astype(bf16)

    def both_cores(x):
        return jnp.roll(jnp.stack([x, to_core(x)], axis=0), h, axis=0).reshape(rows, width)

    layer_out, grad_resid = both_cores(layer_rows), both_cores(pair[1])

    span_keys = keys.shape[0]
    grad_queries, key_parts, value_parts = run_kernel(
        attend_backward,
        (
            jax.ShapeDtypeStruct((tokens, features), bf16),
            jax.ShapeDtypeStruct((span_keys, HEAD_SIZE), f32),
            jax.ShapeDtypeStruct((span_keys, HEAD_SIZE), f32),
        ),
        (queries, keys, values, bias, attn, lse, grad_attn),
        10 * tokens * span_keys * features,
    )
    parts = jnp.stack(
        [key_parts.reshape(SPAN, tokens, HEAD_SIZE), value_parts.reshape(SPAN, tokens, HEAD_SIZE)],
        axis=1,
    )
    total = parts[0]
    for d in range(1, SPAN):
        total = total + lax.ppermute(
            parts[d].astype(bf16), "ctx", [(i, (i - d) % C) for i in range(C)]
        )
    total = total.reshape(2, E, rows, HEAD_SIZE)
    groups = jnp.arange(key_head_array.shape[1] // HEAD_SIZE, dtype=jnp.int32)[None, None, :, None]
    pairs = 0.0
    for j in range(E):
        x = take(total, lax.rem(e + j, E), 1)
        if j:
            x = exp_to(x.astype(bf16), j).astype(f32)
        group = lax.rem(e - j + E, E) * head_count // group_width
        pairs = pairs + jnp.where(groups == group, x[:, :, None, :], 0.0)
    pairs = pairs.astype(bf16).reshape(2, rows, key_head_array.shape[1])
    return layer_out, grad_resid, grad_queries, pairs[0], pairs[1]


def solution(mesh):
    placed = (
        P(("ctx", "exp"), None),
        P("ctx", ("head", "exp")),
        P("ctx", "head"),
        P("ctx", "head"),
        P("ctx"),
        P(("head", "exp"), "ctx"),
        P(),
        P(("ctx", "exp"), None),
        P(("ctx", "exp"), None),
        P(("ctx", "exp"), None, "head"),
        P(("ctx", "exp"), None, "head"),
        P(("ctx", "exp"), "head", None),
        P(("ctx", "exp"), None),
    )
    return jax.shard_map(
        local,
        mesh=mesh,
        in_specs=placed,
        out_specs=(
            P(("ctx", "exp"), None),
            P(("ctx", "exp"), None),
            P("ctx", ("head", "exp")),
            P(("ctx", "exp"), "head"),
            P(("ctx", "exp"), "head"),
        ),
        check_vma=False,
    )
```

```python
import functools
import math

import jax
import jax.numpy as jnp
from jax import lax
from jax.experimental import pallas as pl
from jax.experimental.pallas import tpu as pltpu
from jax.sharding import PartitionSpec as P

HEAD_SIZE = 128
QUERY_HEADS = 64
KEY_VALUE_HEADS = 4
SPAN = 4


neg_large = -1e30
eps_norm = 1e-06
bf16 = jnp.bfloat16
f32 = jnp.float32
SCALE = 1.0 / math.sqrt(HEAD_SIZE)
LAST = (((1,), (1,)), ((), ()))
FIRST = (((0,), (0,)), ((), ()))


def dot(a, b, dims=None):
    if dims is None:
        return jnp.dot(a, b, preferred_element_type=f32)
    return lax.dot_general(a, b, dims, preferred_element_type=f32)


def attend_forward(q_ref, k_ref, v_ref, bias_ref, attn_ref, lse_ref):
    keys, values, bias = k_ref[...], v_ref[...], bias_ref[...]
    totals = []
    for head in range(q_ref.shape[1] // HEAD_SIZE):
        part = slice(head * HEAD_SIZE, (head + 1) * HEAD_SIZE)
        scores = dot(q_ref[:, part], keys, LAST) * SCALE + bias
        top = jnp.max(scores, axis=-1, keepdims=True)
        weights = jnp.exp(scores - top)
        total = jnp.sum(weights, axis=-1, keepdims=True)
        attn_ref[:, part] = (dot(weights.astype(bf16), values) / total).astype(bf16)
        totals.append(top + jnp.log(total))
    lse_ref[...] = jnp.concatenate(totals, axis=1)


def attend_backward(
    q_ref, k_ref, v_ref, bias_ref, attn_ref, lse_ref, grad_ref, dq_ref, dk_ref, dv_ref
):
    keys, values, bias = k_ref[...], v_ref[...], bias_ref[...]
    dk_ref[...] = jnp.zeros_like(dk_ref)
    dv_ref[...] = jnp.zeros_like(dv_ref)
    for head in range(q_ref.shape[1] // HEAD_SIZE):
        part = slice(head * HEAD_SIZE, (head + 1) * HEAD_SIZE)
        query, grad = q_ref[:, part], grad_ref[:, part]
        delta = jnp.sum(
            grad.astype(f32) * attn_ref[:, part].astype(f32), axis=-1, keepdims=True
        )
        scores = dot(query, keys, LAST) * SCALE + bias
        probs = jnp.exp(scores - lse_ref[:, head : head + 1])
        dscore = (probs * (dot(grad, values, LAST) - delta)).astype(bf16)
        dq_ref[:, part] = (dot(dscore, keys) * SCALE).astype(bf16)
        dk_ref[...] += dot(dscore, query, FIRST)
        dv_ref[...] += dot(probs.astype(bf16), grad, FIRST)
    dk_ref[...] = dk_ref[...] * SCALE


def assemble(owner_ref, *refs):
    out_ref = refs[-1]
    for i, ref in enumerate(refs[:-1]):
        out_ref[pl.ds(owner_ref[i], 1)] = ref[...][None]


def join_hidden(
    owner_ref, most_ref, last_ref, residual_ref, gain_ref, hidden_ref, scaled_ref, squares_ref
):
    count = most_ref.shape[0]
    for i in range(count + 1):
        place = pl.ds(owner_ref[i], 1)
        block = most_ref[i : i + 1] if i < count else last_ref[...]
        hidden = residual_ref[place].astype(f32) + block
        hidden_ref[place] = hidden
        scaled_ref[place] = (hidden * gain_ref[...]).astype(bf16)
        squares_ref[place] = jnp.sum(hidden * hidden, axis=-1, keepdims=True)


def expert_middle(count, factor_ref, gates_ref, *refs):
    pre_refs, back_refs = refs[:count], refs[count : 2 * count]
    grads_ref, act_ref, inner_ref = refs[2 * count :]
    rows, ff = back_refs[0].shape
    step = min(rows, 32)
    for j in range(count):

        @pl.loop(0, rows // step)
        def _(i, j=j):
            part = pl.ds(i * step, step)
            into = pl.ds(j * rows + i * step, step)
            factor, gates = factor_ref[into], gates_ref[into]
            gate_raw, up_raw = pre_refs[j][part, :ff], pre_refs[j][part, ff:]
            gate_pre, up_pre = gate_raw * factor, up_raw * factor
            sigma = 1.0 / (1.0 + jnp.exp(-gate_pre))
            silu_val = gate_pre * sigma
            act_ref[into] = (gates * silu_val * up_pre).astype(bf16)
            back_act = gates * back_refs[j][part]
            slope = sigma * (1.0 + gate_pre * (1.0 - sigma))
            grad_gate = (back_act * up_pre * slope).astype(bf16)
            grad_up = (back_act * silu_val).astype(bf16)
            grads_ref[into, :ff] = grad_gate
            grads_ref[into, ff:] = grad_up
            terms = grad_gate.astype(f32) * gate_raw + grad_up.astype(f32) * up_raw
            inner_ref[into] = jnp.sum(terms, axis=-1, keepdims=True)


def run_kernel(body, outs, args, flops, scalars=0):
    moved = sum(a.size * a.dtype.itemsize for a in (*args, *outs))
    in_specs = [pl.BlockSpec(memory_space=pltpu.SMEM)] * scalars
    in_specs += [pl.BlockSpec(memory_space=pltpu.VMEM)] * (len(args) - scalars)
    return pl.pallas_call(
        body,
        out_shape=outs,
        in_specs=in_specs,
        out_specs=tuple(pl.BlockSpec(memory_space=pltpu.VMEM) for _ in outs),
        compiler_params=pltpu.CompilerParams(vmem_limit_bytes=40 * 2**20),
        cost_estimate=pl.CostEstimate(flops=flops, bytes_accessed=moved, transcendentals=0),
    )(*args)


def local(
    residual,
    queries,
    key_head_array,
    value_head_array,
    doc_ids,
    out_weight,
    norm_gain,
    routes,
    gate_probs,
    expert_gate,
    expert_up,
    expert_down,
    grad_out,
):
    C, H, E = lax.axis_size("ctx"), lax.axis_size("head"), lax.axis_size("exp")
    c, h, e = lax.axis_index("ctx"), lax.axis_index("head"), lax.axis_index("exp")
    tokens, features = queries.shape
    head_count = features // HEAD_SIZE
    group_width = QUERY_HEADS // KEY_VALUE_HEADS
    rows, width = residual.shape
    r = rows // H
    cols = width // C
    half = C // 2

    cycle = list(range(0, C, 2)) + list(range(C - 1, 0, -2))
    ahead = [(cycle[i], cycle[(i + 1) % C]) for i in range(C)]
    back = [(d, s) for s, d in ahead]
    odd = lax.rem(c, 2)
    place = c // 2 + odd * (C - c)

    def owner(k):
        at = lax.rem(place + k + C, C)
        return jnp.where(at < half, 2 * at, 2 * (C - at) - 1)

    def after(x, *others):
        return lax.optimization_barrier((x, *others))[0]

    def from_bit(x, bit):
        return lax.ppermute(x, "ctx", [(i, i ^ bit) for i in range(C)])

    def ctx_sum(x, wait):
        for n in range(C.bit_length() - 1):
            x = x + after(from_bit(x, 1 << n), wait[n])
        return x

    def ctx_swap(x):
        bits = C.bit_length() - 1
        shape = x.shape
        x = x.reshape((2,) * bits + shape[1:])
        for axis in range(bits):
            bit = 1 << (bits - 1 - axis)
            mine = jnp.minimum(c & bit, 1)
            got = from_bit(take(x, 1 - mine, axis), bit)
            kept = take(x, mine, axis)
            x = jnp.where(
                mine == 0, jnp.stack([kept, got], axis), jnp.stack([got, kept], axis)
            )
        return x.reshape(shape)

    def in_order(relative, index, axis):
        n = len(relative)
        if n == 2:
            return jnp.where(
                index == 0, jnp.stack(relative, axis), jnp.stack(relative[::-1], axis)
            )
        return jnp.roll(jnp.stack(relative, axis), index, axis=axis)

    def to_ahead(x):
        return lax.ppermute(x, "ctx", ahead)

    def to_back(x):
        return lax.ppermute(x, "ctx", back)

    def to_core(x):
        return lax.ppermute(x, "head", [(i, (i + 1) % H) for i in range(H)])

    def exp_from(x, j):
        return lax.ppermute(x, "exp", [((i + j) % E, i) for i in range(E)])

    def exp_to(x, j):
        return lax.ppermute(x, "exp", [(i, (i + j) % E) for i in range(E)])

    def take(x, i, axis=0):
        return lax.dynamic_index_in_dim(x, i, axis, keepdims=False)

    def ring_gather(x, wait=lambda k, found: None):
        found = {0: x}
        f = b = x
        for k in range(1, half + 1):
            seen = wait(k, found)
            if seen is not None:
                f, b = after((f, b), seen)
            if k < half:
                f, b = to_ahead(f), to_back(b)
                found[-k], found[k] = f, b
        n = x.shape[0] // 2
        found[half] = jnp.concatenate([to_ahead(f[:n]), to_back(b[n:])], axis=0)
        return found

    def ring_reduce(part, arrived=lambda k, sums: None):
        far = part(half, None).astype(bf16)
        n = far.shape[0] // 2
        f, b = to_ahead(far[:n]), to_back(far[n:])
        arrived(half, (f, b))
        seen = None
        for k in range(half - 1, 0, -1):
            own_f, own_b = part(k, seen), part(-k, seen)
            seen = (f, b)
            if k == half - 1:
                own_f = jnp.concatenate([own_f[:n] + f, own_f[n:]], axis=0)
                own_b = jnp.concatenate([own_b[:n], own_b[n:] + b], axis=0)
            else:
                own_f, own_b = own_f + f, own_b + b
            f, b = to_ahead(own_f.astype(bf16)), to_back(own_b.astype(bf16))
            arrived(k, (f, b))
        return part(0, seen) + f + b

    steps = [0] + [sign * k for k in range(1, half) for sign in (-1, 1)] + [half]
    owners = jnp.stack([owner(k) for k in steps]).astype(jnp.int32)

    def in_ctx_order(found):
        out = jax.ShapeDtypeStruct((C,) + found[0].shape, found[0].dtype)
        return run_kernel(assemble, (out,), (owners, *[found[k] for k in steps]), 0, 1)[0]

    pair_index = e * head_count // group_width
    own_keys = lax.dynamic_slice_in_dim(key_head_array, pair_index * HEAD_SIZE, HEAD_SIZE, 1)
    own_values = lax.dynamic_slice_in_dim(value_head_array, pair_index * HEAD_SIZE, HEAD_SIZE, 1)
    docs_rows = jnp.broadcast_to(doc_ids.astype(bf16)[None, :], (16, tokens))
    payload = jnp.concatenate([own_keys, own_values, docs_rows], axis=0)
    blocks = [payload] + [
        lax.ppermute(payload, "ctx", [(i, (i + d) % C) for i in range(C)]) for d in range(1, SPAN)
    ]
    keys = jnp.concatenate([b[:tokens] for b in blocks], axis=0)
    values = jnp.concatenate([b[tokens : 2 * tokens] for b in blocks], axis=0)
    key_docs = jnp.concatenate([b[2 * tokens] for b in blocks], axis=0)
    key_pos = jnp.concatenate(
        [(c - d) * tokens + jnp.arange(tokens, dtype=jnp.int32) for d in range(SPAN)]
    )
    query_pos = c * tokens + jnp.arange(tokens, dtype=jnp.int32)
    visible = (
        (doc_ids.astype(bf16)[:, None] == key_docs[None, :])
        & (key_pos[None, :] <= query_pos[:, None])
        & (key_pos[None, :] >= 0)
    )
    bias = jnp.where(visible, 0.0, neg_large).astype(f32)

    expert_count = C * E
    own_routes, own_gates = take(routes.reshape(H, r, -1), h), take(gate_probs.reshape(H, r, -1), h)
    own_residual = take(residual.reshape(H, r, width), h)
    chosen = own_routes[:, :, None] == jnp.arange(expert_count, dtype=jnp.int32)
    table = jnp.sum(jnp.where(chosen, own_gates[:, :, None], 0.0), axis=1).T.reshape(C, E * r)
    terms, rest = [], table
    for _ in range(3):
        terms.append(lax.reduce_precision(rest, 8, 7))
        rest = rest - terms[-1]
    terms = jnp.concatenate(terms, axis=1).astype(bf16)
    terms = jnp.pad(terms[:, None, :], ((0, 0), (0, 15), (0, cols - terms.shape[1])))
    own_blocks = jnp.swapaxes(own_residual.reshape(r, C, cols), 0, 1)
    swapped = ctx_swap(jnp.concatenate([own_blocks, terms], axis=1))
    residual_cols = swapped[:, :r]
    table = jnp.sum(swapped[:, r, : 3 * E * r].reshape(C, 3, E, r).astype(f32), axis=1)
    gates = [take(table, e, 1)]
    for j in range(1, E):
        gates.append(exp_to(take(table, lax.rem(e + j, E), 1), j))
    gates = [gates[0]] + gates[:0:-1]
    gates = jnp.stack(gates).reshape(E, C * r, 1)

    own_grad_out = take(grad_out.reshape(H, r, width), h)
    grad_found = ring_gather(own_grad_out)
    grads = in_ctx_order(grad_found).reshape(C * r, width)
    grads = [grads] + [exp_from(grads, j) for j in range(1, E)]

    gate_mat, up_mat, down_mat = after((expert_gate[0], expert_up[0], expert_down[0]), bias)
    into = jnp.concatenate([gate_mat, to_core(gate_mat), up_mat, to_core(up_mat)], axis=1)
    down = jnp.concatenate([down_mat, to_core(down_mat)], axis=0)
    ff = down.shape[0]

    attn, lse = run_kernel(
        attend_forward,
        (
            jax.ShapeDtypeStruct((tokens, features), bf16),
            jax.ShapeDtypeStruct((tokens, head_count), f32),
        ),
        (queries, keys, values, bias),
        4 * tokens * keys.shape[0] * features,
    )

    def summed(products):
        kept = jnp.stack([take(x, h, 1) for x in products])
        sent = jnp.stack([take(x, 1 - h, 1).astype(bf16) for x in products])
        share = kept + to_core(sent)
        total = take(share, e, 1)
        for j in range(1, E):
            total = total + exp_to(take(share, lax.rem(e + j, E), 1).astype(bf16), j)
        return total

    def between(k, found):
        if k == 1:
            return [grad_found[1 - half], grad_found[half - 1]]
        return {half - 1: into, half: down}.get(k)

    attn_found = ring_gather(attn, between)
    products = [dot(attn_found[k], out_weight).reshape(E, H, r, cols) for k in steps]
    gain = lax.dynamic_slice_in_dim(norm_gain, c * cols, cols, 0)
    hidden, scaled, squares = run_kernel(
        join_hidden,
        (
            jax.ShapeDtypeStruct((C, r, cols), f32),
            jax.ShapeDtypeStruct((C, r, cols), bf16),
            jax.ShapeDtypeStruct((C, r, 1), f32),
        ),
        (owners, summed(products[:-1]), summed(products[-1:]), residual_cols, gain[None, None]),
        0,
        1,
    )
    scaled = scaled.reshape(C * r, cols)

    found = ring_gather(scaled)
    squares = ctx_sum(squares.reshape(C, r), [(found[k], found[-k]) for k in range(1, half)])
    own_factor = lax.rsqrt(squares / width + eps_norm)
    factor = jnp.stack([own_factor] + [exp_from(own_factor, j) for j in range(1, E)])
    factor = factor.reshape(E, C * r, 1)
    own_factor = own_factor[:, :, None]

    back_raw = [dot(x, down, LAST) for x in grads]

    def times_into(x, k, start=None):
        weight = lax.dynamic_slice_in_dim(into, owner(k) * cols, cols, 0)
        product = dot(x, weight)
        return product if start is None else start + product

    near = half // 2
    arrived = [found]
    for j in range(1, E):
        others = {0: exp_from(scaled, j)}
        for k in range(1, near + 1):
            others[-k], others[k] = to_ahead(others[1 - k]), to_back(others[k - 1])
        if E > 2:
            distant = [k for k in steps if abs(k) > near]
            moved = exp_from(jnp.stack([found[k] for k in distant]), j)
            others.update({k: moved[i] for i, k in enumerate(distant)})
        else:
            others.update({k: exp_from(found[k], j) for k in steps if abs(k) > near})
        arrived.append(others)
    pre = [None] * E
    for k in steps:
        for j in range(E):
            block = arrived[j][k]
            if k == half:
                block = after(block, back_raw[j])
            pre[j] = times_into(block, k, pre[j])

    count = E * C * r
    grad_both, act, inner = run_kernel(
        functools.partial(expert_middle, E),
        (
            jax.ShapeDtypeStruct((count, 2 * ff), bf16),
            jax.ShapeDtypeStruct((count, ff), bf16),
            jax.ShapeDtypeStruct((count, 1), f32),
        ),
        (factor.reshape(count, 1), gates.reshape(count, 1), *pre, *back_raw),
        0,
    )
    inner = inner.reshape(E, C, r)

    def back_part(k, *seen):
        weight = lax.dynamic_slice_in_dim(into, owner(k) * cols, cols, 0)
        left = after(grad_both, *seen) if seen else grad_both
        return dot(left, weight, LAST).reshape(E, C * r, cols)

    def over_exp(k):
        x = back_part(k)
        total = x[0]
        for j in range(1, E):
            total = total + exp_to(x[j].astype(bf16), j)
        return total

    terms = {half: over_exp(half)}
    close = {k: back_part(k) for k in (near, -near)}
    relay = {}
    for j in range(1, E):
        f, b = close[near][j].astype(bf16), close[-near][j].astype(bf16)
        relay[j] = to_ahead(f), to_back(b)
    for k in range(half - 1, near, -1):
        terms[k], terms[-k] = over_exp(k), over_exp(-k)
    close.update({k: back_part(k, terms[half]) for k in range(1 - near, near)})
    extra = []
    for j in range(1, E):
        f, b = relay[j]
        for k in range(near - 1, 0, -1):
            f, b = (close[k][j] + f).astype(bf16), (close[-k][j] + b).astype(bf16)
            f, b = to_ahead(f), to_back(b)
        extra.append(exp_to((close[0][j] + f + b).astype(bf16), j))
    terms[0] = sum(extra, close[0][0])

    act = after(act, relay) if relay else act
    outs = dot(act, down).astype(bf16).reshape(E, C, r, width)
    own_inner = inner[0]
    coming = [exp_to(inner[j], j) for j in range(1, E)]
    bits = [1 << n for n in range(C.bit_length() - 1)]

    def sum_inner(k, sums):
        nonlocal own_inner, coming
        if coming:
            own_inner = sum((after(x, sums) for x in coming), own_inner)
            coming = [from_bit(own_inner, bits.pop())] if bits else []

    def norm_part(k, seen):
        if abs(k) > near or k == 0:
            return terms[k]
        return after(close[k][0], outs) if abs(k) == 1 else close[k][0]

    norm_grad = ring_reduce(norm_part, sum_inner).reshape(C, r, cols)
    inner = own_inner[:, :, None]

    own_grads = lax.dynamic_slice_in_dim(grads[0].reshape(C, r, width), c * cols, cols, 2)
    grad_hidden = (
        own_grads.astype(f32)
        + own_factor * gain * norm_grad
        - hidden * (own_factor * own_factor * own_factor * inner / width)
    )
    grad_cols = grad_hidden.astype(bf16)

    def to_heads(ks, *seen):
        x = jnp.stack([take(grad_cols, owner(k)) for k in ks])
        x = after(x, *seen) if seen else x
        x = in_order([x] + [exp_from(x, j) for j in range(1, E)], e, 1)
        x = in_order([x, to_core(x)], h, 2).reshape(len(ks), tokens, cols)
        return {k: x[i] for i, k in enumerate(ks)}

    first = [half, half - 1, 1 - half]
    grad_rows = to_heads(first)
    grad_rows.update(to_heads([k for k in steps if k not in first]))
    out_sums = {}
    distant = [k for k in steps if abs(k) > near]
    for group in (distant, [k for k in steps if abs(k) <= near]):
        ready = terms[1 - half] if group is distant else list(grad_rows.values())
        for k in group:
            out_sums[k] = take(outs[0], owner(k)).astype(f32)
        for j in range(1, E):
            sent = jnp.stack([take(outs[j], owner(k)) for k in group])
            got = exp_to(after(sent, ready), j)
            for i, k in enumerate(group):
                out_sums[k] = out_sums[k] + got[i]

    grad_attn = ring_reduce(lambda k, seen: dot(grad_rows[k], out_weight, LAST)).astype(bf16)

    def moe_part(k, seen):
        if k == half:
            return after(out_sums[k], norm_grad)
        return after(out_sums[k], grad_attn) if abs(k) == 1 else out_sums[k]

    moe_rows = ring_reduce(moe_part)

    proj = hidden - residual_cols.astype(f32)
    pair = jnp.stack([proj.astype(bf16), grad_cols], axis=1)
    pair = lax.all_to_all(after(pair, grad_attn), "ctx", 0, 0, tiled=True)
    pair = jnp.moveaxis(pair, 0, 2).reshape(2, r, width)
    hidden_rows = own_residual.astype(f32) + pair[0].astype(f32)
    layer_rows = (hidden_rows + moe_rows).astype(bf16)

    def both_cores(x):
        return in_order([x, to_core(x)], h, 0).reshape(rows, width)

    layer_out, grad_resid = both_cores(layer_rows), both_cores(pair[1])

    span_keys = keys.shape[0]
    grad_queries, key_parts, value_parts = run_kernel(
        attend_backward,
        (
            jax.ShapeDtypeStruct((tokens, features), bf16),
            jax.ShapeDtypeStruct((span_keys, HEAD_SIZE), f32),
            jax.ShapeDtypeStruct((span_keys, HEAD_SIZE), f32),
        ),
        (queries, keys, values, bias, attn, lse, grad_attn),
        10 * tokens * span_keys * features,
    )
    parts = jnp.stack(
        [key_parts.reshape(SPAN, tokens, HEAD_SIZE), value_parts.reshape(SPAN, tokens, HEAD_SIZE)],
        axis=1,
    )
    total = parts[0]
    for d in range(1, SPAN):
        total = total + lax.ppermute(
            parts[d].astype(bf16), "ctx", [(i, (i - d) % C) for i in range(C)]
        )
    total = total.reshape(2, E, rows, HEAD_SIZE)
    groups = jnp.arange(key_head_array.shape[1] // HEAD_SIZE, dtype=jnp.int32)[None, None, :, None]
    pairs = 0.0
    for j in range(E):
        x = take(total, lax.rem(e + j, E), 1)
        if j:
            x = exp_to(x.astype(bf16), j).astype(f32)
        group = lax.rem(e - j + E, E) * head_count // group_width
        pairs = pairs + jnp.where(groups == group, x[:, :, None, :], 0.0)
    pairs = pairs.astype(bf16).reshape(2, rows, key_head_array.shape[1])
    return layer_out, grad_resid, grad_queries, pairs[0], pairs[1]


def solution(mesh):
    placed = (
        P(("ctx", "exp"), None),
        P("ctx", ("head", "exp")),
        P("ctx", "head"),
        P("ctx", "head"),
        P("ctx"),
        P(("head", "exp"), "ctx"),
        P(),
        P(("ctx", "exp"), None),
        P(("ctx", "exp"), None),
        P(("ctx", "exp"), None, "head"),
        P(("ctx", "exp"), None, "head"),
        P(("ctx", "exp"), "head", None),
        P(("ctx", "exp"), None),
    )
    return jax.shard_map(
        local,
        mesh=mesh,
        in_specs=placed,
        out_specs=(
            P(("ctx", "exp"), None),
            P(("ctx", "exp"), None),
            P("ctx", ("head", "exp")),
            P(("ctx", "exp"), "head"),
            P(("ctx", "exp"), "head"),
        ),
        check_vma=False,
    )
```

```python
import functools
import math

import jax
import jax.numpy as jnp
from jax import lax
from jax.experimental import pallas as pl
from jax.experimental.pallas import tpu as pltpu
from jax.sharding import PartitionSpec as P

HEAD_SIZE = 128
QUERY_HEADS = 64
KEY_VALUE_HEADS = 4
SPAN = 4


neg_large = -1e30
eps_norm = 1e-06
bf16 = jnp.bfloat16
f32 = jnp.float32
SCALE = 1.0 / math.sqrt(HEAD_SIZE)
LAST = (((1,), (1,)), ((), ()))
FIRST = (((0,), (0,)), ((), ()))


def dot(a, b, dims=None):
    if dims is None:
        return jnp.dot(a, b, preferred_element_type=f32)
    return lax.dot_general(a, b, dims, preferred_element_type=f32)


def attend_forward(q_ref, k_ref, v_ref, bias_ref, attn_ref, lse_ref):
    keys, values, bias = k_ref[...], v_ref[...], bias_ref[...]
    totals = []
    for head in range(q_ref.shape[1] // HEAD_SIZE):
        part = slice(head * HEAD_SIZE, (head + 1) * HEAD_SIZE)
        scores = dot(q_ref[:, part], keys, LAST) * SCALE + bias
        top = jnp.max(scores, axis=-1, keepdims=True)
        weights = jnp.exp(scores - top)
        total = jnp.sum(weights, axis=-1, keepdims=True)
        attn_ref[:, part] = (dot(weights.astype(bf16), values) / total).astype(bf16)
        totals.append(top + jnp.log(total))
    lse_ref[...] = jnp.concatenate(totals, axis=1)


def attend_backward(
    q_ref, k_ref, v_ref, bias_ref, attn_ref, lse_ref, grad_ref, dq_ref, dk_ref, dv_ref
):
    keys, values, bias = k_ref[...], v_ref[...], bias_ref[...]
    dk_ref[...] = jnp.zeros_like(dk_ref)
    dv_ref[...] = jnp.zeros_like(dv_ref)
    for head in range(q_ref.shape[1] // HEAD_SIZE):
        part = slice(head * HEAD_SIZE, (head + 1) * HEAD_SIZE)
        query, grad = q_ref[:, part], grad_ref[:, part]
        delta = jnp.sum(
            grad.astype(f32) * attn_ref[:, part].astype(f32), axis=-1, keepdims=True
        )
        scores = dot(query, keys, LAST) * SCALE + bias
        probs = jnp.exp(scores - lse_ref[:, head : head + 1])
        dscore = (probs * (dot(grad, values, LAST) - delta)).astype(bf16)
        dq_ref[:, part] = (dot(dscore, keys) * SCALE).astype(bf16)
        dk_ref[...] += dot(dscore, query, FIRST)
        dv_ref[...] += dot(probs.astype(bf16), grad, FIRST)
    dk_ref[...] = dk_ref[...] * SCALE


def assemble(owner_ref, *refs):
    out_ref = refs[-1]
    for i, ref in enumerate(refs[:-1]):
        out_ref[pl.ds(owner_ref[i], 1)] = ref[...][None]


def join_hidden(
    owner_ref, most_ref, last_ref, residual_ref, gain_ref, hidden_ref, scaled_ref, squares_ref
):
    count = most_ref.shape[0]
    for i in range(count + 1):
        place = pl.ds(owner_ref[i], 1)
        block = most_ref[i : i + 1] if i < count else last_ref[...]
        hidden = residual_ref[place].astype(f32) + block
        hidden_ref[place] = hidden
        scaled_ref[place] = (hidden * gain_ref[...]).astype(bf16)
        squares_ref[place] = jnp.sum(hidden * hidden, axis=-1, keepdims=True)


def expert_middle(count, factor_ref, gates_ref, *refs):
    pre_refs, back_refs = refs[:count], refs[count : 2 * count]
    grads_ref, act_ref, inner_ref = refs[2 * count :]
    rows, ff = back_refs[0].shape
    step = min(rows, 32)
    for j in range(count):

        @pl.loop(0, rows // step)
        def _(i, j=j):
            part = pl.ds(i * step, step)
            into = pl.ds(j * rows + i * step, step)
            factor, gates = factor_ref[into], gates_ref[into]
            gate_raw, up_raw = pre_refs[j][part, :ff], pre_refs[j][part, ff:]
            gate_pre, up_pre = gate_raw * factor, up_raw * factor
            sigma = 1.0 / (1.0 + jnp.exp(-gate_pre))
            silu_val = gate_pre * sigma
            act_ref[into] = (gates * silu_val * up_pre).astype(bf16)
            back_act = gates * back_refs[j][part]
            slope = sigma * (1.0 + gate_pre * (1.0 - sigma))
            grad_gate = (back_act * up_pre * slope).astype(bf16)
            grad_up = (back_act * silu_val).astype(bf16)
            grads_ref[into, :ff] = grad_gate
            grads_ref[into, ff:] = grad_up
            terms = grad_gate.astype(f32) * gate_raw + grad_up.astype(f32) * up_raw
            inner_ref[into] = jnp.sum(terms, axis=-1, keepdims=True)


def run_kernel(body, outs, args, flops, scalars=0):
    moved = sum(a.size * a.dtype.itemsize for a in (*args, *outs))
    in_specs = [pl.BlockSpec(memory_space=pltpu.SMEM)] * scalars
    in_specs += [pl.BlockSpec(memory_space=pltpu.VMEM)] * (len(args) - scalars)
    return pl.pallas_call(
        body,
        out_shape=outs,
        in_specs=in_specs,
        out_specs=tuple(pl.BlockSpec(memory_space=pltpu.VMEM) for _ in outs),
        compiler_params=pltpu.CompilerParams(vmem_limit_bytes=40 * 2**20),
        cost_estimate=pl.CostEstimate(flops=flops, bytes_accessed=moved, transcendentals=0),
    )(*args)


def local(
    residual,
    queries,
    key_head_array,
    value_head_array,
    doc_ids,
    out_weight,
    norm_gain,
    routes,
    gate_probs,
    expert_gate,
    expert_up,
    expert_down,
    grad_out,
):
    C, H, E = lax.axis_size("ctx"), lax.axis_size("head"), lax.axis_size("exp")
    c, h, e = lax.axis_index("ctx"), lax.axis_index("head"), lax.axis_index("exp")
    tokens, features = queries.shape
    head_count = features // HEAD_SIZE
    group_width = QUERY_HEADS // KEY_VALUE_HEADS
    rows, width = residual.shape
    r = rows // H
    cols = width // C
    half = C // 2

    cycle = list(range(0, C, 2)) + list(range(C - 1, 0, -2))
    ahead = [(cycle[i], cycle[(i + 1) % C]) for i in range(C)]
    back = [(d, s) for s, d in ahead]
    odd = lax.rem(c, 2)
    place = c // 2 + odd * (C - c)

    def owner(k):
        at = lax.rem(place + k + C, C)
        return jnp.where(at < half, 2 * at, 2 * (C - at) - 1)

    def after(x, *others):
        return lax.optimization_barrier((x, *others))[0]

    def from_bit(x, bit):
        return lax.ppermute(x, "ctx", [(i, i ^ bit) for i in range(C)])

    def ctx_sum(x, wait):
        for n in range(C.bit_length() - 1):
            x = x + after(from_bit(x, 1 << n), wait[n])
        return x

    def ctx_swap(x):
        bits = C.bit_length() - 1
        shape = x.shape
        x = x.reshape((2,) * bits + shape[1:])
        for axis in range(bits):
            bit = 1 << (bits - 1 - axis)
            mine = jnp.minimum(c & bit, 1)
            got = from_bit(take(x, 1 - mine, axis), bit)
            kept = take(x, mine, axis)
            x = jnp.where(
                mine == 0, jnp.stack([kept, got], axis), jnp.stack([got, kept], axis)
            )
        return x.reshape(shape)

    def in_order(relative, index, axis):
        n = len(relative)
        if n == 2:
            return jnp.where(
                index == 0, jnp.stack(relative, axis), jnp.stack(relative[::-1], axis)
            )
        return jnp.roll(jnp.stack(relative, axis), index, axis=axis)

    def to_ahead(x):
        return lax.ppermute(x, "ctx", ahead)

    def to_back(x):
        return lax.ppermute(x, "ctx", back)

    def to_core(x):
        return lax.ppermute(x, "head", [(i, (i + 1) % H) for i in range(H)])

    def exp_from(x, j):
        return lax.ppermute(x, "exp", [((i + j) % E, i) for i in range(E)])

    def exp_to(x, j):
        return lax.ppermute(x, "exp", [(i, (i + j) % E) for i in range(E)])

    def take(x, i, axis=0):
        return lax.dynamic_index_in_dim(x, i, axis, keepdims=False)

    def ring_gather(x, wait=lambda k, found: None):
        found = {0: x}
        f = b = x
        for k in range(1, half + 1):
            seen = wait(k, found)
            if seen is not None:
                f, b = after((f, b), seen)
            if k < half:
                f, b = to_ahead(f), to_back(b)
                found[-k], found[k] = f, b
        n = x.shape[0] // 2
        found[half] = jnp.concatenate([to_ahead(f[:n]), to_back(b[n:])], axis=0)
        return found

    def ring_reduce(part, arrived=lambda k, sums: None):
        far = part(half, None).astype(bf16)
        n = far.shape[0] // 2
        f, b = to_ahead(far[:n]), to_back(far[n:])
        arrived(half, (f, b))
        seen = None
        for k in range(half - 1, 0, -1):
            own_f, own_b = part(k, seen), part(-k, seen)
            seen = (f, b)
            if k == half - 1:
                own_f = jnp.concatenate([own_f[:n] + f, own_f[n:]], axis=0)
                own_b = jnp.concatenate([own_b[:n], own_b[n:] + b], axis=0)
            else:
                own_f, own_b = own_f + f, own_b + b
            f, b = to_ahead(own_f.astype(bf16)), to_back(own_b.astype(bf16))
            arrived(k, (f, b))
        return part(0, seen) + f + b

    steps = [0] + [sign * k for k in range(1, half) for sign in (-1, 1)] + [half]
    owners = jnp.stack([owner(k) for k in steps]).astype(jnp.int32)

    def in_ctx_order(found):
        out = jax.ShapeDtypeStruct((C,) + found[0].shape, found[0].dtype)
        return run_kernel(assemble, (out,), (owners, *[found[k] for k in steps]), 0, 1)[0]

    pair_index = e * head_count // group_width
    own_keys = lax.dynamic_slice_in_dim(key_head_array, pair_index * HEAD_SIZE, HEAD_SIZE, 1)
    own_values = lax.dynamic_slice_in_dim(value_head_array, pair_index * HEAD_SIZE, HEAD_SIZE, 1)
    docs_rows = jnp.broadcast_to(doc_ids.astype(bf16)[None, :], (16, tokens))
    payload = jnp.concatenate([own_keys, own_values, docs_rows], axis=0)
    blocks = [payload] + [
        lax.ppermute(payload, "ctx", [(i, (i + d) % C) for i in range(C)]) for d in range(1, SPAN)
    ]
    keys = jnp.concatenate([b[:tokens] for b in blocks], axis=0)
    values = jnp.concatenate([b[tokens : 2 * tokens] for b in blocks], axis=0)
    key_docs = jnp.concatenate([b[2 * tokens] for b in blocks], axis=0)
    key_pos = jnp.concatenate(
        [(c - d) * tokens + jnp.arange(tokens, dtype=jnp.int32) for d in range(SPAN)]
    )
    query_pos = c * tokens + jnp.arange(tokens, dtype=jnp.int32)
    visible = (
        (doc_ids.astype(bf16)[:, None] == key_docs[None, :])
        & (key_pos[None, :] <= query_pos[:, None])
        & (key_pos[None, :] >= 0)
    )
    bias = jnp.where(visible, 0.0, neg_large).astype(f32)

    expert_count = C * E
    own_routes, own_gates = take(routes.reshape(H, r, -1), h), take(gate_probs.reshape(H, r, -1), h)
    own_residual = take(residual.reshape(H, r, width), h)
    chosen = own_routes[:, :, None] == jnp.arange(expert_count, dtype=jnp.int32)
    table = jnp.sum(jnp.where(chosen, own_gates[:, :, None], 0.0), axis=1).T.reshape(C, E * r)
    terms, rest = [], table
    for _ in range(3):
        terms.append(lax.reduce_precision(rest, 8, 7))
        rest = rest - terms[-1]
    terms = jnp.concatenate(terms, axis=1).astype(bf16)
    terms = jnp.pad(terms[:, None, :], ((0, 0), (0, 15), (0, cols - terms.shape[1])))
    own_blocks = jnp.swapaxes(own_residual.reshape(r, C, cols), 0, 1)
    swapped = ctx_swap(jnp.concatenate([own_blocks, terms], axis=1))
    residual_cols = swapped[:, :r]
    table = jnp.sum(swapped[:, r, : 3 * E * r].reshape(C, 3, E, r).astype(f32), axis=1)
    gates = [take(table, e, 1)]
    for j in range(1, E):
        gates.append(exp_to(take(table, lax.rem(e + j, E), 1), j))
    gates = [gates[0]] + gates[:0:-1]
    gates = jnp.stack(gates).reshape(E, C * r, 1)

    own_grad_out = take(grad_out.reshape(H, r, width), h)
    grad_found = ring_gather(own_grad_out)
    grads = in_ctx_order(grad_found).reshape(C * r, width)
    grads = [grads] + [exp_from(grads, j) for j in range(1, E)]

    gate_mat, up_mat, down_mat = after((expert_gate[0], expert_up[0], expert_down[0]), bias)
    into = jnp.concatenate([gate_mat, to_core(gate_mat), up_mat, to_core(up_mat)], axis=1)
    down = jnp.concatenate([down_mat, to_core(down_mat)], axis=0)
    ff = down.shape[0]

    attn, lse = run_kernel(
        attend_forward,
        (
            jax.ShapeDtypeStruct((tokens, features), bf16),
            jax.ShapeDtypeStruct((tokens, head_count), f32),
        ),
        (queries, keys, values, bias),
        4 * tokens * keys.shape[0] * features,
    )

    def summed(products):
        kept = jnp.stack([take(x, h, 1) for x in products])
        sent = jnp.stack([take(x, 1 - h, 1).astype(bf16) for x in products])
        share = kept + to_core(sent)
        total = take(share, e, 1)
        for j in range(1, E):
            total = total + exp_to(take(share, lax.rem(e + j, E), 1).astype(bf16), j)
        return total

    def between(k, found):
        if k == 1:
            return [grad_found[1 - half], grad_found[half - 1]]
        return {half - 1: into, half: down}.get(k)

    attn_found = ring_gather(attn, between)
    products = [dot(attn_found[k], out_weight).reshape(E, H, r, cols) for k in steps]
    gain = lax.dynamic_slice_in_dim(norm_gain, c * cols, cols, 0)
    hidden, scaled, squares = run_kernel(
        join_hidden,
        (
            jax.ShapeDtypeStruct((C, r, cols), f32),
            jax.ShapeDtypeStruct((C, r, cols), bf16),
            jax.ShapeDtypeStruct((C, r, 1), f32),
        ),
        (owners, summed(products[:-1]), summed(products[-1:]), residual_cols, gain[None, None]),
        0,
        1,
    )
    scaled = scaled.reshape(C * r, cols)

    found = ring_gather(scaled)
    squares = ctx_sum(squares.reshape(C, r), [(found[k], found[-k]) for k in range(1, half)])
    own_factor = lax.rsqrt(squares / width + eps_norm)
    factor = jnp.stack([own_factor] + [exp_from(own_factor, j) for j in range(1, E)])
    factor = factor.reshape(E, C * r, 1)
    own_factor = own_factor[:, :, None]

    back_raw = [dot(x, down, LAST) for x in grads]

    def times_into(x, k, start=None):
        weight = lax.dynamic_slice_in_dim(into, owner(k) * cols, cols, 0)
        product = dot(x, weight)
        return product if start is None else start + product

    near = half // 2
    arrived = [found]
    for j in range(1, E):
        others = {0: exp_from(scaled, j)}
        for k in range(1, near + 1):
            others[-k], others[k] = to_ahead(others[1 - k]), to_back(others[k - 1])
        if E > 2:
            distant = [k for k in steps if abs(k) > near]
            moved = exp_from(jnp.stack([found[k] for k in distant]), j)
            others.update({k: moved[i] for i, k in enumerate(distant)})
        else:
            others.update({k: exp_from(found[k], j) for k in steps if abs(k) > near})
        arrived.append(others)
    pre = [None] * E
    for k in steps:
        for j in range(E):
            block = arrived[j][k]
            if k == half:
                block = after(block, back_raw[j])
            pre[j] = times_into(block, k, pre[j])

    count = E * C * r
    grad_both, act, inner = run_kernel(
        functools.partial(expert_middle, E),
        (
            jax.ShapeDtypeStruct((count, 2 * ff), bf16),
            jax.ShapeDtypeStruct((count, ff), bf16),
            jax.ShapeDtypeStruct((count, 1), f32),
        ),
        (factor.reshape(count, 1), gates.reshape(count, 1), *pre, *back_raw),
        0,
    )
    inner = inner.reshape(E, C, r)

    def back_part(k, *seen):
        weight = lax.dynamic_slice_in_dim(into, owner(k) * cols, cols, 0)
        left = after(grad_both, *seen) if seen else grad_both
        return dot(left, weight, LAST).reshape(E, C * r, cols)

    def over_exp(k):
        x = back_part(k)
        total = x[0]
        for j in range(1, E):
            total = total + exp_to(x[j].astype(bf16), j)
        return total

    terms = {half: over_exp(half)}
    close = {k: back_part(k) for k in (near, -near)}
    relay = {}
    for j in range(1, E):
        f, b = close[near][j].astype(bf16), close[-near][j].astype(bf16)
        relay[j] = to_ahead(f), to_back(b)
    for k in range(half - 1, near, -1):
        terms[k], terms[-k] = over_exp(k), over_exp(-k)
    close.update({k: back_part(k, terms[half]) for k in range(1 - near, near)})
    extra = []
    for j in range(1, E):
        f, b = relay[j]
        for k in range(near - 1, 0, -1):
            f, b = (close[k][j] + f).astype(bf16), (close[-k][j] + b).astype(bf16)
            f, b = to_ahead(f), to_back(b)
        extra.append(exp_to((close[0][j] + f + b).astype(bf16), j))
    terms[0] = sum(extra, close[0][0])

    act = after(act, relay) if relay else act
    outs = dot(act, down).astype(bf16).reshape(E, C, r, width)
    own_inner = inner[0]
    coming = [exp_to(inner[j], j) for j in range(1, E)]
    bits = [1 << n for n in range(C.bit_length() - 1)]

    def sum_inner(k, sums):
        nonlocal own_inner, coming
        if coming:
            own_inner = sum((after(x, sums) for x in coming), own_inner)
            coming = [from_bit(own_inner, bits.pop())] if bits else []

    def norm_part(k, seen):
        if abs(k) > near or k == 0:
            return terms[k]
        return after(close[k][0], outs) if abs(k) == 1 else close[k][0]

    norm_grad = ring_reduce(norm_part, sum_inner).reshape(C, r, cols)
    inner = own_inner[:, :, None]

    own_grads = lax.dynamic_slice_in_dim(grads[0].reshape(C, r, width), c * cols, cols, 2)
    grad_hidden = (
        own_grads.astype(f32)
        + own_factor * gain * norm_grad
        - hidden * (own_factor * own_factor * own_factor * inner / width)
    )
    grad_cols = grad_hidden.astype(bf16)

    def to_heads(ks, *seen):
        x = jnp.stack([take(grad_cols, owner(k)) for k in ks])
        x = after(x, *seen) if seen else x
        x = in_order([x] + [exp_from(x, j) for j in range(1, E)], e, 1)
        x = in_order([x, to_core(x)], h, 2).reshape(len(ks), tokens, cols)
        return {k: x[i] for i, k in enumerate(ks)}

    first = [half, half - 1, 1 - half]
    grad_rows = to_heads(first)
    grad_rows.update(to_heads([k for k in steps if k not in first]))
    out_sums = {}
    distant = [k for k in steps if abs(k) > near]
    for group in (distant, [k for k in steps if abs(k) <= near]):
        ready = terms[1 - half] if group is distant else list(grad_rows.values())
        for k in group:
            out_sums[k] = take(outs[0], owner(k)).astype(f32)
        for j in range(1, E):
            sent = jnp.stack([take(outs[j], owner(k)) for k in group])
            got = exp_to(after(sent, ready), j)
            for i, k in enumerate(group):
                out_sums[k] = out_sums[k] + got[i]

    grad_attn = ring_reduce(lambda k, seen: dot(grad_rows[k], out_weight, LAST)).astype(bf16)

    def moe_part(k, seen):
        if abs(k) > near:
            return after(out_sums[k], norm_grad)
        return after(out_sums[k], grad_attn) if abs(k) == 1 else out_sums[k]

    moe_seen = {}
    moe_rows = ring_reduce(moe_part, moe_seen.__setitem__)

    proj = hidden - residual_cols.astype(f32)
    pair = jnp.stack([proj.astype(bf16), grad_cols], axis=1)
    pair = lax.all_to_all(after(pair, grad_attn), "ctx", 0, 0, tiled=True)
    pair = jnp.moveaxis(pair, 0, 2).reshape(2, r, width)
    hidden_rows = own_residual.astype(f32) + pair[0].astype(f32)
    layer_rows = (hidden_rows + moe_rows).astype(bf16)

    def both_cores(x):
        return in_order([x, to_core(x)], h, 0).reshape(rows, width)

    layer_out, grad_resid = both_cores(layer_rows), both_cores(pair[1])

    span_keys = keys.shape[0]
    grad_queries, key_parts, value_parts = run_kernel(
        attend_backward,
        (
            jax.ShapeDtypeStruct((tokens, features), bf16),
            jax.ShapeDtypeStruct((span_keys, HEAD_SIZE), f32),
            jax.ShapeDtypeStruct((span_keys, HEAD_SIZE), f32),
        ),
        (queries, keys, values, bias, attn, lse, grad_attn),
        10 * tokens * span_keys * features,
    )
    parts = jnp.stack(
        [key_parts.reshape(SPAN, tokens, HEAD_SIZE), value_parts.reshape(SPAN, tokens, HEAD_SIZE)],
        axis=1,
    )
    parts = after(parts, moe_seen[near])
    total = parts[0]
    for d in range(1, SPAN):
        total = total + lax.ppermute(
            parts[d].astype(bf16), "ctx", [(i, (i - d) % C) for i in range(C)]
        )
    total = total.reshape(2, E, rows, HEAD_SIZE)
    groups = jnp.arange(key_head_array.shape[1] // HEAD_SIZE, dtype=jnp.int32)[None, None, :, None]
    pairs = 0.0
    for j in range(E):
        x = take(total, lax.rem(e + j, E), 1)
        if j:
            x = exp_to(x.astype(bf16), j).astype(f32)
        group = lax.rem(e - j + E, E) * head_count // group_width
        pairs = pairs + jnp.where(groups == group, x[:, :, None, :], 0.0)
    pairs = pairs.astype(bf16).reshape(2, rows, key_head_array.shape[1])
    return layer_out, grad_resid, grad_queries, pairs[0], pairs[1]


def solution(mesh):
    placed = (
        P(("ctx", "exp"), None),
        P("ctx", ("head", "exp")),
        P("ctx", "head"),
        P("ctx", "head"),
        P("ctx"),
        P(("head", "exp"), "ctx"),
        P(),
        P(("ctx", "exp"), None),
        P(("ctx", "exp"), None),
        P(("ctx", "exp"), None, "head"),
        P(("ctx", "exp"), None, "head"),
        P(("ctx", "exp"), "head", None),
        P(("ctx", "exp"), None),
    )
    return jax.shard_map(
        local,
        mesh=mesh,
        in_specs=placed,
        out_specs=(
            P(("ctx", "exp"), None),
            P(("ctx", "exp"), None),
            P("ctx", ("head", "exp")),
            P(("ctx", "exp"), "head"),
            P(("ctx", "exp"), "head"),
        ),
        check_vma=False,
    )
```
